32 devices in a mesh: dp: 16 (over z, x, core), tp: 2 (over y).
Axes of the slice: x: 2, y: 2, z: 4, core: 2. Of those that a mesh axis runs over, the one named last changes fastest.
Arguments:
- layer_in: float32 [75264, 512], P(('dp', 'tp')), may hold values from -6 to 6
- out_grad: float32 [75264, 512], P(('dp', 'tp')), may hold values from -6 to 6
- w_qkv: bfloat16 [512, 1536], P('dp', 'tp'), may hold values from -0.25 to 0.25
- b_qv: bfloat16 [1024], P('dp'), may hold values from -3 to 3
- w_proj: bfloat16 [512, 512], P('tp', 'dp'), may hold values from -1 to 1
- b_proj: bfloat16 [512], P('dp'), may hold values from -3 to 3
- w_fc1: bfloat16 [512, 2048], P('dp', 'tp'), may hold values from -0.25 to 0.25
- b_fc1: bfloat16 [2048], P('dp'), may hold values from -3 to 3
- w_fc2: bfloat16 [2048, 512], P('tp', 'dp'), may hold values from -0.25 to 0.25
- b_fc2: bfloat16 [512], P('dp'), may hold values from -3 to 3
- gain_one: bfloat16 [512], P('dp'), may hold values from 0.099609375 to 1.8984375
- shift_one: bfloat16 [512], P('dp'), may hold values from -3 to 3
- gain_two: bfloat16 [512], P('dp'), may hold values from 0.099609375 to 1.8984375
- shift_two: bfloat16 [512], P('dp'), may hold values from -3 to 3
- rel_table: bfloat16 [16, 169], replicated, may hold values from -4 to 4
- rel_index: int32 [49, 49], replicated, may hold values from 0 to 168, as said below
Outputs:
- layer_out: float32 [75264, 512], P(('dp', 'tp'))
- in_grad: float32 [75264, 512], P(('dp', 'tp'))
- grad_w_qkv: float32 [512, 1536], P('dp', 'tp')
- grad_b_qv: float32 [1024], P('dp')
- grad_w_proj: float32 [512, 512], P('tp', 'dp')
- grad_b_proj: float32 [512], P('dp')
- grad_w_fc1: float32 [512, 2048], P('dp', 'tp')
- grad_b_fc1: float32 [2048], P('dp')
- grad_w_fc2: float32 [2048, 512], P('tp', 'dp')
- grad_b_fc2: float32 [512], P('dp')
- grad_gain_one: float32 [512], P('dp')
- grad_shift_one: float32 [512], P('dp')
- grad_gain_two: float32 [512], P('dp')
- grad_shift_two: float32 [512], P('dp')
- grad_rel_table: float32 [16, 169], replicated
The draws below stay inside these ranges and needn't reach their ends.
Inputs may be any that keep to these rules, and one draw needn't show every extreme that they name: `rel_index`: entry [i, j] depends only on the row offset and the column offset between place i and place j of a 7 x 7 window, and different offset pairs have different entries.
All inputs are finite; a program needn't handle non-finite values.
Results may differ from the reference program's by a relative error of at most 0.017.
Values may be sent and summed in bfloat16 or wider, within the bound.
A program may use at most 320 MiB of HBM per device.

```python
import jax
import jax.numpy as jnp
from jax import lax

D = 512
HEADS = 16
HEAD_DIM = 32
FF = 2048
IMG_TP = 12
RES = 14
WIN = 7
SHIFT = 3
TBL = 169
TOKENS = 75264


def draw_rel_index(key, part):
    key = jax.random.fold_in(key, 11)
    labels = jax.random.permutation(key, TBL).astype(jnp.int32)
    places = jnp.arange(WIN * WIN, dtype=jnp.int32)
    row_of = places // WIN
    col_of = places % WIN
    offset = (row_of[:, None] - row_of[None, :] + WIN - 1) * (2 * WIN - 1) + (col_of[:, None] - col_of[None, :] + WIN - 1)
    return labels[offset]


def raised(drawn, rng, source, target, blocks, factor):
    def block_of(dim):
        return (jnp.arange(drawn.shape[dim]) // (drawn.shape[dim] // blocks)).reshape((-1,) + (1,) * (drawn.ndim - 1 - dim))

    first = jax.random.permutation(rng, blocks)[block_of(target)]
    far = (block_of(target) + blocks // 2) % blocks
    return jnp.where((block_of(source) == first) | (block_of(source) == far), factor * drawn, drawn)


def shard_levels(key, dims, shards, least, largest):
    level = 1.0
    for dim, parts in shards:
        heights = jax.random.uniform(jax.random.fold_in(jax.random.fold_in(key, 6), dim), (parts,), jnp.float32, least / len(shards), largest / len(shards))
        level = level * jnp.repeat(jnp.exp(heights), dims[dim] // parts).reshape((-1,) + (1,) * (len(dims) - 1 - dim))
    return level


def noise(key, shape, deviation, reach, split=(), kind=jnp.bfloat16):
    level = shard_levels(key, shape, split, -0.22, 0.18) if split else 1.0
    values = jax.random.normal(key, shape, jnp.float32) * deviation * level
    return jnp.minimum(jnp.maximum(values, -reach), reach).astype(kind)


def heavy_noise(own_key, extent, scale, bound, cuts, heavy, held_as=jnp.bfloat16):
    values = scale * jax.random.normal(own_key, extent, jnp.float32)
    if cuts:
        values = values * shard_levels(own_key, extent, cuts, -0.22, 0.18)
    return jnp.clip(raised(values, jax.random.fold_in(own_key, 3), *heavy), -bound, bound).astype(held_as)


def setup_inputs(seed: int = 0) -> dict:
    seeds = jax.random.split(jax.random.key(seed), 17)
    return {
        "layer_in": noise(seeds[0], (TOKENS, D), 1.0, 6.0, ((0, 32),), jnp.float32),
        "out_grad": heavy_noise(seeds[1], (TOKENS, D), 1.0, 6.0, ((0, 32),), (0, 1, 32, 2.75), jnp.float32),
        "w_qkv": noise(seeds[2], (D, 3 * D), D ** -0.5, 0.25, ((0, 16), (1, 2))),
        "b_qv": noise(seeds[3], (2 * D,), 0.5, 3.0, ((0, 16),)),
        "w_proj": noise(seeds[4], (D, D), (D // 16) ** -0.5, 1.0, ((0, 2), (1, 16))),
        "b_proj": noise(seeds[5], (D,), 0.5, 3.0, ((0, 16),)),
        "w_fc1": noise(seeds[6], (D, FF), D ** -0.5, 0.25, ((0, 16), (1, 2))),
        "b_fc1": noise(seeds[7], (FF,), 0.5, 3.0, ((0, 16),)),
        "w_fc2": noise(seeds[8], (FF, D), (FF // 4) ** -0.5, 0.25, ((0, 2), (1, 16))),
        "b_fc2": noise(seeds[9], (D,), 0.5, 3.0, ((0, 16),)),
        "gain_one": jnp.clip(1.0 + 0.18 * jax.random.normal(seeds[10], (D,), jnp.float32), 0.099609375, 1.8984375).astype(jnp.bfloat16),
        "shift_one": noise(seeds[11], (D,), 0.5, 3.0, ((0, 16),)),
        "gain_two": jnp.clip(1.0 + 0.18 * jax.random.normal(seeds[12], (D,), jnp.float32), 0.099609375, 1.8984375).astype(jnp.bfloat16),
        "shift_two": noise(seeds[13], (D,), 0.5, 3.0, ((0, 16),)),
        "rel_table": noise(seeds[14], (HEADS, TBL), 1.0, 4.0),
        "rel_index": draw_rel_index(jax.random.fold_in(seeds[16], 71), 0),
    }


HIGHEST = lax.Precision.HIGHEST

@jax.custom_vjp
def low(v):
    return lax.optimization_barrier(v.astype(jnp.bfloat16)).astype(jnp.float32)

@jax.custom_vjp
def low_back(v):
    return v

def low_keep(v):
    return (low(v), None)

def low_pass(kept, grad):
    return (grad,)

def back_keep(v):
    return (v, None)

def back_low(kept, grad):
    return (low(grad),)
low.defvjp(low_keep, low_pass)
low_back.defvjp(back_keep, back_low)

def layer_norm(tensor, gain, shift):
    average = lax.optimization_barrier(jnp.mean(tensor, axis=-1, keepdims=True))
    centred = tensor - average
    spread = lax.optimization_barrier(jnp.mean(centred * centred, axis=-1, keepdims=True))
    return centred * lax.rsqrt(spread + 1e-05) * gain + shift

def to_windows(tensor, images):
    per_side = RES // WIN
    inner = tensor.shape[1:]
    lattice = tensor.reshape((images, RES, RES) + inner)
    lattice = jnp.roll(lattice, (-SHIFT, -SHIFT), axis=(1, 2))
    lattice = lattice.reshape((images, per_side, WIN, per_side, WIN) + inner)
    lattice = jnp.swapaxes(lattice, 2, 3)
    return lattice.reshape((images * per_side * per_side, WIN * WIN) + inner)

def from_windows(tensor, images):
    per_side = RES // WIN
    inner = tensor.shape[2:]
    lattice = tensor.reshape((images, per_side, per_side, WIN, WIN) + inner)
    lattice = jnp.swapaxes(lattice, 2, 3).reshape((images, RES, RES) + inner)
    lattice = jnp.roll(lattice, (SHIFT, SHIFT), axis=(1, 2))
    return lattice.reshape((images * RES * RES,) + inner)

def window_masks():
    per_side = RES // WIN
    places = jnp.arange(RES, dtype=jnp.int32)
    band_of = (places >= RES - WIN).astype(jnp.int32) + (places >= RES - SHIFT).astype(jnp.int32)
    labels = band_of[:, None] * 3 + band_of[None, :]
    labels = labels.reshape(per_side, WIN, per_side, WIN)
    labels = jnp.swapaxes(labels, 1, 2).reshape(per_side * per_side, WIN * WIN)
    return jnp.where(labels[:, :, None] != labels[:, None, :], -100.0, 0.0).astype(jnp.float32)

def forward(layer_in, w_qkv, b_qv, w_proj, b_proj, w_fc1, b_fc1, w_fc2, b_fc2, gain_one, shift_one, gain_two, shift_two, rel_table, rel_index):
    images = layer_in.shape[0] // (RES * RES)
    per_image = (RES // WIN) ** 2
    normed = low(layer_norm(layer_in, gain_one, shift_one))
    project = jnp.dot(normed, w_qkv, precision=HIGHEST).reshape(-1, HEADS, 3, HEAD_DIM)
    biases = b_qv.reshape(HEADS, 2, HEAD_DIM)
    queries = low(low_back(project[:, :, 0] + biases[:, 0]))
    keys_only = low(low_back(project[:, :, 1]))
    values = low(low_back(project[:, :, 2] + biases[:, 1]))
    query_win = to_windows(queries, images)
    key_win = to_windows(keys_only, images)
    value_win = to_windows(values, images)
    scores = jnp.einsum('wqhd,wkhd->whqk', query_win, key_win, precision=HIGHEST) * HEAD_DIM ** (-0.5)
    offsets = rel_table[:, rel_index]
    masks = window_masks()
    shaped = scores.reshape((images, per_image) + scores.shape[1:]) + offsets[None, None] + masks[None, :, None]
    scores = low_back(shaped.reshape(scores.shape))
    probs = low(jax.nn.softmax(scores, axis=-1))
    mixed = jnp.einsum('whqk,wkhd->wqhd', probs, value_win, precision=HIGHEST)
    mixed = low(low_back(from_windows(mixed, images).reshape(-1, D)))
    middle = layer_in + low_back(jnp.dot(mixed, w_proj, precision=HIGHEST)) + b_proj
    normed_two = low(layer_norm(middle, gain_two, shift_two))
    hidden = low_back(jnp.dot(normed_two, w_fc1, precision=HIGHEST) + b_fc1)
    active = low(jax.nn.gelu(hidden, approximate=False))
    return middle + low_back(jnp.dot(active, w_fc2, precision=HIGHEST)) + b_fc2

def reference(layer_in, out_grad, w_qkv, b_qv, w_proj, b_proj, w_fc1, b_fc1, w_fc2, b_fc2, gain_one, shift_one, gain_two, shift_two, rel_table, rel_index):
    params = tuple((member.astype(jnp.float32) for member in (w_qkv, b_qv, w_proj, b_proj, w_fc1, b_fc1, w_fc2, b_fc2, gain_one, shift_one, gain_two, shift_two, rel_table)))
    group_rows = 2 * IMG_TP * RES * RES
    blocks_in = layer_in.astype(jnp.float32).reshape(-1, group_rows, D)
    blocks_grad = out_grad.astype(jnp.float32).reshape(-1, group_rows, D)

    def one_group(totals, both_blocks):
        block_in, block_grad = both_blocks

        def run_layer(tensor, *weights):
            return forward(tensor, *weights, rel_index)
        result, pullback = jax.vjp(run_layer, block_in, *params)
        gradients = pullback(block_grad)
        totals = tuple((carried + fresh for carried, fresh in zip(totals, gradients[1:])))
        return (totals, (result, gradients[0]))
    zeros = tuple((jnp.zeros(member.shape, jnp.float32) for member in params))
    totals, (outputs, in_grads) = lax.scan(one_group, zeros, (blocks_in, blocks_grad))
    return (outputs.reshape(-1, D), in_grads.reshape(-1, D), totals[0], totals[1], totals[2], totals[3], totals[4], totals[5], totals[6], totals[7], totals[8], totals[9], totals[10], totals[11], totals[12])
```

```python
import functools

import jax
import jax.numpy as jnp
from jax import lax
from jax.experimental import pallas as pl
from jax.experimental.pallas import tpu as pltpu
from jax.sharding import PartitionSpec as P

D = 512
HEADS = 16
HEAD_DIM = 32
FF = 2048
RES = 14
WIN = 7
SHIFT = 3
TBL = 169
PLACES = WIN * WIN
PAD = 64
PAIR = 2
ROWS = PAIR * RES * RES
WROWS = PAIR * 4 * PAD
GROUPS = 4
LANES = 128
SCALE = HEAD_DIM ** (-0.5)
QKV, PROJ, FC1, FC2 = 0, 768, 1024, 2048
COLS = 3072
CHUNK = 512
EPS = 1e-05
HIGHEST = lax.Precision.HIGHEST


def dot(left, right, dims=(1, 0)):
    return lax.dot_general(
        left, right, (((dims[0],), (dims[1],)), ((), ())), preferred_element_type=jnp.float32
    )


def row_sum(value):
    return jnp.sum(value, axis=0, keepdims=True)


def norm_parts(value):
    centred = value - jnp.mean(value, axis=-1, keepdims=True)
    inverse = lax.rsqrt(jnp.mean(centred * centred, axis=-1, keepdims=True) + EPS)
    return centred * inverse, inverse


def norm_back(upstream, hat, inverse, gain):
    scaled = upstream * gain
    return (
        scaled
        - jnp.mean(scaled, axis=-1, keepdims=True)
        - hat * jnp.mean(scaled * hat, axis=-1, keepdims=True)
    ) * inverse


def pick_heads(stacked):
    lane = lax.broadcasted_iota(jnp.int32, (PAD, LANES), 1)
    parts = [stacked[h * PAD : (h + 1) * PAD] for h in range(4)]
    low = jnp.where(lane < 32, parts[0], parts[1])
    high = jnp.where(lane < 96, parts[2], parts[3])
    return jnp.where(lane < 64, low, high)


def block_kernel(
    x_ref, og_ref, w_ref, vec_ref, b1_ref, bias_ref, to_win_ref, to_tok_ref, hm_ref,
    out_ref, ig_ref, gw_ref, gvec_ref, gb1_ref, gtab_ref,
    acc_ref, qkv_ref, mixw_ref, probs_ref, pg_ref, dmw_ref, nw_ref, mo_ref, dn_ref,
):
    bf16, f32 = jnp.bfloat16, jnp.float32
    step = pl.program_id(0)

    @pl.when(step == 0)
    def _():
        acc_ref[...] = jnp.zeros_like(acc_ref)
        gvec_ref[...] = jnp.zeros_like(gvec_ref)
        gb1_ref[...] = jnp.zeros_like(gb1_ref)
        gtab_ref[...] = jnp.zeros_like(gtab_ref)

    def vec(row):
        return vec_ref[row : row + 1, :]

    hat, _ = norm_parts(x_ref[...])
    normed = (hat * vec(4) + vec(5)).astype(bf16)
    nw_ref[...] = dot(to_win_ref[...], normed).astype(bf16)
    for t in range(2):
        half = slice(t * 256, t * 256 + 256)
        project = dot(nw_ref[...], w_ref[t, :, QKV:PROJ])
        qkv_ref[t, :, 0:256] = (project[:, 0:256] + vec_ref[0:1, half]).astype(bf16)
        qkv_ref[t, :, 256:512] = project[:, 256:512].astype(bf16)
        qkv_ref[t, :, 512:768] = (project[:, 512:768] + vec_ref[1:2, half]).astype(bf16)

    def spread(value):
        return jnp.concatenate([value] * 4, axis=0) * hm_ref[...]

    @pl.loop(0, PAIR * 4)
    def _(w):
        rows = pl.ds(pl.multiple_of(w * PAD, PAD), PAD)
        place = lax.rem(w, 4)
        for g in range(GROUPS):
            t, base = g // 2, (g % 2) * LANES
            q = spread(qkv_ref[t, rows, base : base + LANES])
            k = qkv_ref[t, rows, 256 + base : 256 + base + LANES]
            v = qkv_ref[t, rows, 512 + base : 512 + base + LANES]
            scores = dot(q, k, (1, 1)) * SCALE + bias_ref[place, g]
            powers = jnp.exp(scores - jnp.max(scores, axis=-1, keepdims=True))
            probs = powers * (1.0 / jnp.sum(powers, axis=-1, keepdims=True))
            probs_ref[w, g] = probs
            mixed = pick_heads(dot(probs.astype(bf16), v))
            mixw_ref[rows, g * LANES : (g + 1) * LANES] = mixed.astype(bf16)

    mix = dot(to_tok_ref[...], mixw_ref[...]).astype(bf16)
    attn = dot(mix[:, 0:256], w_ref[0, :, PROJ:FC1], (1, 1)) + dot(
        mix[:, 256:512], w_ref[1, :, PROJ:FC1], (1, 1)
    )
    middle = x_ref[...] + attn + vec(2)
    hat2, inverse2 = norm_parts(middle)
    normed_two = (hat2 * vec(6) + vec(7)).astype(bf16)
    out_low = og_ref[...].astype(bf16)
    mo_ref[...] = middle + vec(3)
    dn_ref[...] = jnp.zeros_like(dn_ref)

    @pl.loop(0, 2)
    def _(t):
        for j in range(1024 // CHUNK):
            one = slice(FC1 + j * CHUNK, FC1 + (j + 1) * CHUNK)
            two = slice(FC2 + j * CHUNK, FC2 + (j + 1) * CHUNK)
            cols = slice(j * CHUNK, (j + 1) * CHUNK)
            hidden = dot(normed_two, w_ref[t, :, one]) + b1_ref[t, :, cols]
            cdf = 0.5 + 0.5 * lax.erf(hidden * (0.5**0.5))
            active = (hidden * cdf).astype(bf16)
            mo_ref[...] += dot(active, w_ref[t, :, two], (1, 1))
            slope = cdf + hidden * (jnp.exp(hidden * hidden * -0.5) * 0.3989422804014327)
            hidden_grad = (dot(out_low, w_ref[t, :, two]) * slope).astype(bf16)
            dn_ref[...] += dot(hidden_grad, w_ref[t, :, one], (1, 1))
            acc_ref[t, :, two] += dot(out_low, active, (0, 0))
            acc_ref[t, :, one] += dot(normed_two, hidden_grad, (0, 0))
            gb1_ref[t, :, cols] += row_sum(hidden_grad.astype(f32))

    out_ref[...] = mo_ref[...]
    upstream = dn_ref[...]
    out_grad = og_ref[...]
    middle_grad = out_grad + norm_back(upstream, hat2, inverse2, vec(6))
    mo_ref[...] = middle_grad
    gvec_ref[2:3, :] += row_sum(middle_grad)
    gvec_ref[3:4, :] += row_sum(out_grad)
    gvec_ref[6:7, :] += row_sum(upstream * hat2)
    gvec_ref[7:8, :] += row_sum(upstream)
    middle_low = middle_grad.astype(bf16)
    middle_win = dot(to_win_ref[...], middle_low).astype(bf16)
    for t in range(2):
        half = slice(t * 256, t * 256 + 256)
        dmw_ref[:, half] = dot(middle_win, w_ref[t, :, PROJ:FC1]).astype(bf16)
        acc_ref[t, :, PROJ:FC1] += dot(middle_low, mix[:, half], (0, 0))

    @pl.loop(0, PAIR * 4)
    def _(w):
        rows = pl.ds(pl.multiple_of(w * PAD, PAD), PAD)
        for g in range(GROUPS):
            t, base = g // 2, (g % 2) * LANES
            q = spread(qkv_ref[t, rows, base : base + LANES])
            k = qkv_ref[t, rows, 256 + base : 256 + base + LANES]
            v = qkv_ref[t, rows, 512 + base : 512 + base + LANES]
            up = spread(dmw_ref[rows, g * LANES : (g + 1) * LANES])
            probs = probs_ref[w, g]
            probs_grad = dot(up, v, (1, 1))
            weighted = jnp.sum(probs * probs_grad, axis=-1, keepdims=True)
            score_grad = (probs * (probs_grad - weighted)).astype(bf16)
            gtab_ref[g] += score_grad.astype(f32)
            dq = pick_heads(dot(score_grad, k)) * SCALE
            dk = dot(score_grad, q, (0, 0)) * SCALE
            dv = dot(probs.astype(bf16), up, (0, 0))
            pg_ref[t, rows, base : base + LANES] = dq.astype(bf16)
            pg_ref[t, rows, 256 + base : 256 + base + LANES] = dk.astype(bf16)
            pg_ref[t, rows, 512 + base : 512 + base + LANES] = dv.astype(bf16)

    for t in range(2):
        half = slice(t * 256, t * 256 + 256)
        acc_ref[t, :, QKV:PROJ] += dot(nw_ref[...], pg_ref[t], (0, 0))
        gvec_ref[0:1, half] += row_sum(pg_ref[t, :, 0:256].astype(f32))
        gvec_ref[1:2, half] += row_sum(pg_ref[t, :, 512:768].astype(f32))
    back = dot(pg_ref[0], w_ref[0, :, QKV:PROJ], (1, 1)) + dot(
        pg_ref[1], w_ref[1, :, QKV:PROJ], (1, 1)
    )
    upstream = dot(to_tok_ref[...], back.astype(bf16))
    hat, inverse = norm_parts(x_ref[...])
    gvec_ref[4:5, :] += row_sum(upstream * hat)
    gvec_ref[5:6, :] += row_sum(upstream)
    ig_ref[...] = mo_ref[...] + norm_back(upstream, hat, inverse, vec(4))

    @pl.when(step == pl.num_programs(0) - 1)
    def _():
        gw_ref[...] = acc_ref[...].astype(bf16)


def run_block(layer_in, out_grad, weights, vecs, bias_one, bias, to_win, to_tok, head_mask):
    rows = layer_in.shape[0]
    bf16, f32 = jnp.bfloat16, jnp.float32

    def whole(shape):
        return pl.BlockSpec(shape, lambda i: (0,) * len(shape), pipeline_mode=pl.Buffered(1))

    tokens = pl.BlockSpec((ROWS, D), lambda i: (i, 0))
    fixed = (weights, vecs, bias_one, bias, to_win, to_tok, head_mask)
    outs = (
        jax.ShapeDtypeStruct((rows, D), f32),
        jax.ShapeDtypeStruct((rows, D), f32),
        jax.ShapeDtypeStruct((2, D, COLS), bf16),
        jax.ShapeDtypeStruct((8, D), f32),
        jax.ShapeDtypeStruct((2, 1, FF // 2), f32),
        jax.ShapeDtypeStruct((GROUPS, 4 * PAD, PAD), f32),
    )
    return pl.pallas_call(
        block_kernel,
        grid=(rows // ROWS,),
        out_shape=outs,
        in_specs=[tokens, tokens] + [whole(member.shape) for member in fixed],
        out_specs=[tokens, tokens] + [whole(member.shape) for member in outs[2:]],
        scratch_shapes=[
            pltpu.VMEM((2, D, COLS), f32),
            pltpu.VMEM((2, WROWS, 768), bf16),
            pltpu.VMEM((WROWS, D), bf16),
            pltpu.VMEM((PAIR * 4, GROUPS, 4 * PAD, PAD), f32),
            pltpu.VMEM((2, WROWS, 768), bf16),
            pltpu.VMEM((WROWS, D), bf16),
            pltpu.VMEM((WROWS, D), bf16),
            pltpu.VMEM((ROWS, D), f32),
            pltpu.VMEM((ROWS, D), f32),
        ],
        compiler_params=pltpu.CompilerParams(
            dimension_semantics=("arbitrary",), vmem_limit_bytes=60 * 1024 * 1024
        ),
    )(layer_in, out_grad, *fixed)


def window_source():
    spot = jnp.arange(WROWS, dtype=jnp.int32)
    image, window, place = spot // (4 * PAD), (spot // PAD) % 4, spot % PAD
    row = ((window // 2) * WIN + place // WIN + SHIFT) % RES
    col = ((window % 2) * WIN + place % WIN + SHIFT) % RES
    return jnp.where(place < PLACES, image * RES * RES + row * RES + col, -1)


def score_bias(table, rel_index):
    places = jnp.arange(RES, dtype=jnp.int32)
    band_of = (places >= RES - WIN).astype(jnp.int32) + (places >= RES - SHIFT).astype(jnp.int32)
    labels = (band_of[:, None] * 3 + band_of[None, :]).reshape(2, WIN, 2, WIN)
    labels = jnp.swapaxes(labels, 1, 2).reshape(4, PLACES)
    masks = jnp.where(labels[:, :, None] != labels[:, None, :], -100.0, 0.0).astype(jnp.float32)
    gap = PAD - PLACES
    index = jnp.pad(rel_index, ((0, gap), (0, gap)), constant_values=-1).reshape(-1)
    onehot = (index[:, None] == jnp.arange(TBL, dtype=jnp.int32)[None, :]).astype(jnp.bfloat16)
    offsets = dot(table, onehot, (1, 1)).reshape(HEADS, PAD, PAD)
    masks = jnp.pad(masks, ((0, 0), (0, gap), (0, gap)))
    absent = jnp.where(jnp.arange(PAD) < PLACES, 0.0, -1e30).astype(jnp.float32)
    bias = offsets[None] + masks[:, None] + absent
    return bias.reshape(4, GROUPS, 4 * PAD, PAD), onehot


def per_device(
    layer_in, out_grad, w_qkv, b_qv, w_proj, b_proj, w_fc1, b_fc1, w_fc2, b_fc2,
    gain_one, shift_one, gain_two, shift_two, rel_table, rel_index,
):
    dp_size = lax.axis_size("dp")
    dp_here = lax.axis_index("dp")
    tp_size = lax.axis_size("tp")
    part = w_qkv.shape[0]
    both = ("dp", "tp")
    qkv_cols = w_qkv.reshape(part, 8, 3, HEAD_DIM).swapaxes(1, 2).reshape(part, 768)
    vectors = (b_qv, b_proj, b_fc2, gain_one, shift_one, gain_two, shift_two, b_fc1)
    small = jnp.concatenate(vectors).reshape(part, -1)
    small = jnp.pad(small, ((0, 0), (0, LANES - small.shape[1])))
    packed = jnp.concatenate((qkv_cols, w_proj.T, w_fc1, w_fc2.T, small), axis=1)
    spread = lax.all_gather(packed, both, axis=0, tiled=False)
    spread = spread.reshape(dp_size, tp_size, part, COLS + LANES)
    weights = spread[..., :COLS].swapaxes(0, 1).reshape(tp_size, D, COLS)
    flat = spread[:, 0, :, COLS : COLS + 12].reshape(dp_size, part * 12).astype(jnp.float32)
    pieces = []
    start = 0
    for vector in vectors:
        size = vector.shape[0]
        pieces.append(flat[:, start : start + size].reshape(-1))
        start += size
    qv = pieces[0].reshape(HEADS, 2, HEAD_DIM)
    vecs = jnp.stack((qv[:, 0].reshape(-1), qv[:, 1].reshape(-1), *pieces[1:7]))
    bias, onehot = score_bias(rel_table, rel_index)
    source = window_source()
    to_win = (source[:, None] == jnp.arange(ROWS, dtype=jnp.int32)[None, :]).astype(jnp.bfloat16)
    to_tok = (source[None, :] == jnp.arange(ROWS, dtype=jnp.int32)[:, None]).astype(jnp.bfloat16)
    head_mask = (
        jnp.arange(4 * PAD, dtype=jnp.int32)[:, None] // PAD
        == jnp.arange(LANES, dtype=jnp.int32)[None, :] // HEAD_DIM
    ).astype(jnp.bfloat16)
    layer_out, in_grad, gw, gvec, gb1, gtab = run_block(
        layer_in, out_grad, weights, vecs, pieces[7].reshape(2, 1, FF // 2), bias,
        to_win, to_tok, head_mask,
    )
    ready = gw.reshape(tp_size, dp_size, part, COLS).swapaxes(0, 1).reshape(-1, COLS)
    mine = lax.psum_scatter(ready, both, scatter_dimension=0, tiled=True).astype(jnp.float32)
    grad_qkv = mine[:, QKV:PROJ].reshape(part, 3, 8, HEAD_DIM).swapaxes(1, 2).reshape(part, 768)
    table_grad = lax.dot_general(
        gtab.reshape(HEADS, PAD * PAD),
        onehot.astype(jnp.float32),
        (((1,), (0,)), ((), ())),
        precision=HIGHEST,
        preferred_element_type=jnp.float32,
    )
    bundle = jnp.concatenate((gvec.reshape(-1), gb1.reshape(-1), table_grad.reshape(-1)))
    bundle = jnp.pad(bundle, (0, -bundle.shape[0] % 1024)).reshape(-1, LANES)
    total = jnp.sum(lax.all_gather(bundle, both, axis=0, tiled=False), axis=0).reshape(-1)
    rows = total[: 8 * D].reshape(8, D)
    qv_grad = jnp.stack(
        (rows[0].reshape(HEADS, HEAD_DIM), rows[1].reshape(HEADS, HEAD_DIM)), axis=1
    ).reshape(-1)

    def shard(vector):
        size = vector.shape[0] // dp_size
        return lax.dynamic_slice_in_dim(vector, dp_here * size, size)

    return (
        layer_out,
        in_grad,
        grad_qkv,
        shard(qv_grad),
        mine[:, PROJ:FC1].T,
        shard(rows[2]),
        mine[:, FC1:FC2],
        shard(total[8 * D : 8 * D + FF]),
        mine[:, FC2:COLS].T,
        shard(rows[3]),
        shard(rows[4]),
        shard(rows[5]),
        shard(rows[6]),
        shard(rows[7]),
        total[8 * D + FF : 8 * D + FF + HEADS * TBL].reshape(HEADS, TBL),
    )


def solution(mesh):
    tokens = P(("dp", "tp"), None)
    vector = P("dp")
    in_specs = (
        tokens, tokens, P("dp", "tp"), vector, P("tp", "dp"), vector, P("dp", "tp"), vector,
        P("tp", "dp"), vector, vector, vector, vector, vector, P(), P(),
    )
    out_specs = (
        tokens, tokens, P("dp", "tp"), vector, P("tp", "dp"), vector, P("dp", "tp"), vector,
        P("tp", "dp"), vector, vector, vector, vector, vector, P(),
    )
    return jax.shard_map(
        per_device, mesh=mesh, in_specs=in_specs, out_specs=out_specs, check_vma=False
    )
```
